32 devices in a mesh: dp: 4 (over y, core), tensor: 8 (over z, x).
Axes of the slice: x: 2, y: 2, z: 4, core: 2. Of those that a mesh axis runs over, the one named last changes fastest.
Arguments:
- gate_pre: bfloat16 [28, 512, 4096], P(None, 'tensor', 'dp'), parts along dimension 2, may hold values from -6 to 6
- up_pre: bfloat16 [28, 512, 4096], P(None, 'tensor', 'dp'), parts along dimension 2, may hold values from -6 to 6
- down_weight: bfloat16 [28, 512, 4096], P(None, 'tensor'), may hold values from -0.0625 to 0.0625
Outputs:
- mixed: bfloat16 [4096, 4096], P('tensor', 'dp'), parts along dimension 1
The draws below stay inside these ranges and needn't reach their ends.
There are 4 independent parts, one for each index of `dp`. The reference program is written for one: setup_inputs(seed, part) draws one part's arguments, and reference() takes and returns one part's arrays. A program takes and returns all parts, laid end to end along the dimension named above; an argument that names none is the same for every part. Nothing has to cross between parts.
All inputs are finite; a program needn't handle non-finite values.
Results may differ from the reference program's by a relative error of at most 0.024.
Values may be sent and summed in bfloat16 or wider, within the bound.
No kernel may reach another device: no remote copies, remote signals or barrier semaphores. Data moves between devices by JAX's collectives and lax.ppermute only.
A program may use at most 128 MiB of HBM per device.

```python
import math
import jax
import jax.numpy as jnp
import numpy as np
from jax import lax

HF = 28
HB = 512
DOUT = 4096
TOK = 1024
FF = 14336
N_TENSOR = 8


def strengthened(values, stream_key, source, target, blocks, factor):
    def block_of(axis_at):
        return (jnp.arange(values.shape[axis_at]) // (values.shape[axis_at] // blocks)).reshape((-1,) + (1,) * (values.ndim - 1 - axis_at))

    near = jax.random.permutation(stream_key, blocks)[block_of(target)]
    far = (block_of(target) + blocks // 2) % blocks
    return jnp.where((block_of(source) == near) | (block_of(source) == far), factor * values, values)


def levels(rng, shape, pieces, least, high):
    factor_of, own = 1.0, jax.random.fold_in(rng, 6)
    for axis_at, parts in pieces:
        steps = jnp.exp(jax.random.uniform(jax.random.fold_in(own, axis_at), (parts,), jnp.float32, least / len(pieces), high / len(pieces)))
        factor_of = factor_of * jnp.repeat(steps, shape[axis_at] // parts).reshape([-1 if axis == axis_at else 1 for axis in range(len(shape))])
    return factor_of


def scatter_about(rng, dims, deviation, most, split=(), dtype=jnp.bfloat16):
    result = deviation * jax.random.normal(rng, dims, jnp.float32)
    if split:
        result = result * levels(rng, dims, split, -0.22, 0.18)
    return jnp.clip(result, -most, most).astype(dtype)


def bell_draw_with(key, extent, deviation, bound, split, heavy, held_as=jnp.bfloat16):
    drawn = deviation * jax.random.normal(key, extent, jnp.float32)
    if split:
        drawn = drawn * levels(key, extent, split, -0.22, 0.18)
    return jnp.clip(strengthened(drawn, jax.random.fold_in(key, 3), *heavy), -bound, bound).astype(held_as)


def setup_inputs(seed: int = 0, part: int = 0) -> dict:
    seeds = jax.random.split(jax.random.key(seed), 4)
    part_splits = jax.random.split(jax.random.fold_in(seeds[3], part), 4)
    gate_pre = scatter_about(part_splits[0], (HF, HB, TOK), 1.0, 6.0, ((1, 8),))
    up_pre = scatter_about(part_splits[1], (HF, HB, TOK), 1.0, 6.0, ((1, 8),))
    down_weight = bell_draw_with(seeds[2], (HF, HB, DOUT), FF ** -0.5, 0.0625, ((1, 8),), (1, 2, 8, 2.0))
    return dict(gate_pre=gate_pre, up_pre=up_pre, down_weight=down_weight)


def character(value, prime_order):
    residue = value % prime_order
    if residue == 0:
        return 0
    squares_list = [index * index % prime_order for index in range(1, prime_order)]
    return 1 if residue in squares_list else -1

def paley_matrix():
    prime_order = 13
    conference = np.zeros((14, 14))
    conference[0, 1:] = 1.0
    conference[1:, 0] = 1.0
    for row_index in range(prime_order):
        for col_index in range(prime_order):
            conference[row_index + 1, col_index + 1] = character(col_index - row_index, prime_order)
    first = np.array([[1.0, 1.0], [1.0, -1.0]])
    second = np.array([[1.0, -1.0], [-1.0, -1.0]])
    return np.kron(conference, first) + np.kron(np.eye(14), second)

def sylvester(order):
    matrix = np.ones((1, 1))
    basic = np.array([[1.0, 1.0], [1.0, -1.0]])
    while matrix.shape[0] < order:
        matrix = np.kron(basic, matrix)
    return matrix

def reference(gate_pre, up_pre, down_weight):
    hidden = (jax.nn.silu(gate_pre.astype(jnp.float32)) * up_pre.astype(jnp.float32)).astype(jnp.bfloat16)
    left_factor = jnp.asarray(paley_matrix(), jnp.float32)
    right_factor = jnp.asarray(sylvester(HB), jnp.float32)
    transformed = jnp.einsum('ij,jbt->ibt', left_factor, hidden.astype(jnp.float32), precision=lax.Precision.DEFAULT)
    transformed = jnp.einsum('bc,act->abt', right_factor, transformed, precision=lax.Precision.HIGH)
    rotated = (transformed * (1.0 / math.sqrt(HF * HB))).astype(jnp.bfloat16)
    group_width = HB // N_TENSOR
    total = jnp.zeros((DOUT, TOK), jnp.float32)
    for block_index in range(N_TENSOR):
        rot_rows = rotated[:, block_index * group_width:(block_index + 1) * group_width, :].reshape(HF * group_width, TOK)
        weight_rows = down_weight[:, block_index * group_width:(block_index + 1) * group_width, :].reshape(HF * group_width, DOUT)
        partial_value = lax.dot_general(weight_rows, rot_rows, (((0,), (0,)), ((), ())), preferred_element_type=jnp.float32)
        partial_value = lax.optimization_barrier(partial_value.astype(jnp.bfloat16)).astype(jnp.float32)
        total = total + partial_value
    return total.astype(jnp.bfloat16)
```

```python
import functools
import math

import jax
import jax.numpy as jnp
import numpy as np
from jax import lax
from jax.experimental import pallas as pl
from jax.experimental.pallas import tpu as pltpu
from jax.sharding import PartitionSpec as P

CHUNKS = 8
VMEM = 48 * 1024 * 1024
ORDER = (1, 2, 3, 4, 5, 6, 0)


def character(value, prime_order):
    residue = value % prime_order
    if residue == 0:
        return 0
    squares_list = [index * index % prime_order for index in range(1, prime_order)]
    return 1 if residue in squares_list else -1


def paley_matrix():
    prime_order = 13
    conference = np.zeros((14, 14))
    conference[0, 1:] = 1.0
    conference[1:, 0] = 1.0
    for row_index in range(prime_order):
        for col_index in range(prime_order):
            conference[row_index + 1, col_index + 1] = character(col_index - row_index, prime_order)
    first = np.array([[1.0, 1.0], [1.0, -1.0]])
    second = np.array([[1.0, -1.0], [-1.0, -1.0]])
    return np.kron(conference, first) + np.kron(np.eye(14), second)


def sylvester(order):
    matrix = np.ones((1, 1))
    basic = np.array([[1.0, 1.0], [1.0, -1.0]])
    while matrix.shape[0] < order:
        matrix = np.kron(basic, matrix)
    return matrix


def exchange(value, bit):
    pairs = [(source, source ^ (1 << bit)) for source in range(lax.axis_size("tensor"))]
    return lax.ppermute(value, "tensor", pairs)


def call(kernel, after, operands, specs, outs, out_specs, grid, flops, scratch=()):
    moved = sum(int(np.prod(x.shape)) * x.dtype.itemsize for x in (*operands, *outs))

    def run(_, *refs):
        kernel(*refs)

    return pl.pallas_call(
        run,
        out_shape=outs,
        grid=grid,
        in_specs=[pl.BlockSpec(memory_space=pl.ANY), *specs],
        out_specs=out_specs,
        scratch_shapes=list(scratch),
        compiler_params=pltpu.CompilerParams(vmem_limit_bytes=VMEM),
        cost_estimate=pl.CostEstimate(flops=flops, bytes_accessed=moved, transcendentals=0),
    )(after, *operands)


def bf16(*shape):
    return jax.ShapeDtypeStruct(shape, jnp.bfloat16)


def rows_spec(rows, step, offset=0):
    return pl.BlockSpec((rows, step), lambda i: (i + offset, 0))


SCALAR = pl.BlockSpec(memory_space=pltpu.SMEM)


def activate(after, gate, up, chunk, step):
    units = gate.shape[0]
    blocks = 4

    def kernel(gate_ref, up_ref, out_ref):
        g = gate_ref[...].astype(jnp.float32)
        u = up_ref[...].astype(jnp.float32)
        out_ref[...] = (g / (1.0 + jnp.exp(-g)) * u).astype(jnp.bfloat16)

    spec = pl.BlockSpec((units // blocks, step), lambda i: (i, chunk))
    return call(
        kernel, after, (gate, up), [spec, spec], [bf16(units, step)],
        [rows_spec(units // blocks, step)], (blocks,), 0,
    )[0]


def mix(after, partner, own, sign):
    units, step = own.shape
    blocks = 2

    def kernel(partner_ref, own_ref, sign_ref, out_ref):
        total = partner_ref[...].astype(jnp.float32) + sign_ref[0] * own_ref[...].astype(jnp.float32)
        out_ref[...] = total.astype(jnp.bfloat16)

    spec = rows_spec(units // blocks, step)
    return call(
        kernel, after, (partner, own, sign), [spec, spec, SCALAR], [bf16(units, step)],
        [spec], (blocks,), 0,
    )[0]


def fold_weight(after, weight, factor, block_of, scale, first, count, devices):
    units, features = weight.shape
    rows = features // devices

    def kernel(block_ref, _, weight_ref, factor_ref, out_ref):
        product = lax.dot_general(
            weight_ref[...], factor_ref[...], (((0,), (0,)), ((), ())),
            preferred_element_type=jnp.float32,
        )
        out_ref[...] = (product * scale).astype(jnp.bfloat16)

    return pl.pallas_call(
        kernel,
        out_shape=bf16(count * rows, units),
        grid_spec=pltpu.PrefetchScalarGridSpec(
            num_scalar_prefetch=1,
            grid=(count,),
            in_specs=[
                pl.BlockSpec(memory_space=pl.ANY),
                pl.BlockSpec((units, rows), lambda i, block: (0, block[first + i])),
                pl.BlockSpec((units, units), lambda i, block: (0, 0)),
            ],
            out_specs=pl.BlockSpec((rows, units), lambda i, block: (i, 0)),
        ),
        compiler_params=pltpu.CompilerParams(vmem_limit_bytes=VMEM),
        cost_estimate=pl.CostEstimate(
            flops=2 * count * rows * units * units,
            bytes_accessed=2 * units * (2 * count * rows + units),
            transcendentals=0,
        ),
    )(block_of, after, weight, factor)


def project(after, partner, own, sign, given_weight, kept_weight):
    units, step = own.shape
    half = given_weight.shape[0]
    blocks = 4
    rows = half // blocks

    def kernel(partner_ref, own_ref, sign_ref, given_w, kept_w, given_ref, kept_ref, mixed):
        index = pl.program_id(0)

        @pl.when(index == 0)
        def _():
            total = partner_ref[...].astype(jnp.float32) + sign_ref[0] * own_ref[...].astype(jnp.float32)
            mixed[...] = total.astype(jnp.bfloat16)

        @pl.when(index < blocks)
        def _():
            given_ref[...] = jnp.dot(
                given_w[...], mixed[...], preferred_element_type=jnp.float32
            ).astype(jnp.bfloat16)

        @pl.when(index >= blocks)
        def _():
            kept_ref[...] = jnp.dot(
                kept_w[...], mixed[...], preferred_element_type=jnp.float32
            ).astype(jnp.bfloat16)

    whole = pl.BlockSpec((units, step), lambda i: (0, 0))
    early = lambda i: (jnp.minimum(i, blocks - 1), 0)
    late = lambda i: (jnp.maximum(i - blocks, 0), 0)
    return call(
        kernel, after, (partner, own, sign, given_weight, kept_weight),
        [whole, whole, SCALAR, pl.BlockSpec((rows, units), early), pl.BlockSpec((rows, units), late)],
        [bf16(half, step), bf16(half, step)],
        [pl.BlockSpec((rows, step), early), pl.BlockSpec((rows, step), late)],
        (2 * blocks,), 4 * half * units * step, [pltpu.VMEM((units, step), jnp.bfloat16)],
    )


def add(after, taken, kept):
    rows, step = kept.shape

    def kernel(taken_ref, kept_ref, out_ref):
        total = taken_ref[...].astype(jnp.float32) + kept_ref[...].astype(jnp.float32)
        out_ref[...] = total.astype(jnp.bfloat16)

    spec = rows_spec(rows, step)
    return call(kernel, after, (taken, kept), [spec, spec], [bf16(rows, step)], [spec], (1,), 0)[0]


def add_split(after, taken, kept):
    rows, step = kept.shape
    half = rows // 2

    def kernel(taken_ref, kept_ref, given_ref, kept_out):
        total = taken_ref[...].astype(jnp.float32) + kept_ref[...].astype(jnp.float32)
        total = total.astype(jnp.bfloat16)
        kept_out[...] = total[:half]
        given_ref[...] = total[half:]

    spec = rows_spec(rows, step)
    out = rows_spec(half, step)
    return call(
        kernel, after, (taken, kept), [spec, spec], [bf16(half, step)] * 2, [out, out], (1,), 0
    )


def body(gate_pre, up_pre, down_weight):
    left, width, tokens = gate_pre.shape
    units = left * width
    features = down_weight.shape[-1]
    devices = lax.axis_size("tensor")
    levels = devices.bit_length() - 1
    position = lax.axis_index("tensor")
    signs = [
        (1 - 2 * ((position >> level) & 1)).astype(jnp.float32).reshape(1) for level in range(levels)
    ]
    scale = 1.0 / math.sqrt(units * devices)
    factor = jnp.asarray(np.kron(paley_matrix(), sylvester(width)), jnp.bfloat16)
    weight = down_weight.reshape(units, features)
    gate = gate_pre.reshape(units, tokens)
    up = up_pre.reshape(units, tokens)
    step = tokens // CHUNKS

    order = sorted(
        range(devices),
        key=lambda r: (1 - (r & 1), *[(r >> level) & 1 for level in range(1, levels)]),
    )
    block_of = jnp.asarray(order, jnp.int32) ^ position

    last = [gate]
    folded = []
    half = devices // 2

    def fold(part):
        parts = 4 if devices >= 8 else 2
        count = devices // parts
        made = fold_weight(
            last[0], weight, factor, block_of, scale, part * count, count, devices
        )
        last[0] = made
        folded.append(made)

    state = [None] * CHUNKS
    outs = [None] * CHUNKS
    stages = 2 * levels + 1

    def weights():
        if len(folded) != 2:
            both = [jnp.concatenate(folded[:2]), jnp.concatenate(folded[2:])]
            folded[:] = both
        return folded

    def run(stage, chunk):
        if stage == 0:
            made = activate(last[0], gate, up, chunk, step)
            last[0] = made
            state[chunk] = (exchange(made, 0), made)
            return
        partner, own = state[chunk]
        if stage < levels:
            made = mix(last[0], partner, own, signs[stage - 1])
            last[0] = made
            state[chunk] = (exchange(made, stage), made)
        elif stage == levels:
            given, kept = project(last[0], partner, own, signs[stage - 1], *weights())
            last[0] = kept
            state[chunk] = (exchange(given, 0), kept)
        elif stage < 2 * levels:
            given, kept = add_split(last[0], partner, own)
            last[0] = kept
            state[chunk] = (exchange(given, stage - levels), kept)
        else:
            outs[chunk] = last[0] = add(last[0], partner, own)

    run(0, 0)
    fold(0)
    run(0, 1)
    for turn in range(1, CHUNKS + stages):
        for stage in range(1, stages):
            chunk = turn - stage
            if 0 <= chunk < CHUNKS:
                run(stage, chunk)
        if turn + 1 < CHUNKS:
            run(0, turn + 1)
        if len(folded) < 4 and turn < levels:
            fold(len(folded))
            if turn == levels - 1:
                while len(folded) < 4:
                    fold(len(folded))
    return jnp.concatenate(outs, axis=1)


def solution(mesh):
    in_specs = (P(None, "tensor", "dp"), P(None, "tensor", "dp"), P(None, "tensor", None))
    out_specs = P("tensor", "dp")
    return jax.shard_map(body, mesh=mesh, in_specs=in_specs, out_specs=out_specs, check_vma=False)
```

```python
import math

import jax
import jax.numpy as jnp
import numpy as np
from jax import lax
from jax.experimental import pallas as pl
from jax.experimental.pallas import tpu as pltpu
from jax.sharding import PartitionSpec as P

SIZES = (1, 1, 1, 1, 1, 1, 1, 1)
EXCHANGE = (
    (2, 0, 1), (1, 0, 2), (0, 1, 2), (1, 0, 2), (0, 1, 2), (0, 1, 2), (1, 0, 2), (2, 1, 0),
)
REDUCE = (
    (0, 1, 2), (0, 1, 2), (0, 1, 2), (0, 1, 2), (0, 1, 2), (0, 1, 2), (0, 2, 1), (0, 1, 2),
)
EVENTS = (
    3, 7, 4, 1, 3, 6, 2, 7, 0, 4, 5, 1, 3, 0, 5, 6, 1, 2, 3, 7, 0, 6, 4, 1,
    7, 3, 5, 4, 1, 2, 6, 7, 4, 0, 2, 3, 6, 1, 5, 4, 6, 0, 4, 7, 3, 5, 0, 7,
    2, 5, 0, 2, 5, 1, 6, 2,
)
COSTS = (
    1, 1, 1, 1, 1, 1, 1, 1,
    1, 1, 1, 1, 1, 1, 1, 1,
    1, 1, 1, 1, 1, 1, 1, 1,
    1, 1, 1, 1, 1, 1, 1, 1,
    1, 1, 1, 1, 1, 1, 1, 1,
    1, 1, 1, 1, 1, 1, 1, 1,
    1, 1, 1, 1, 1, 1, 1, 1,
)
VMEM = 48 * 1024 * 1024


def character(value, prime_order):
    residue = value % prime_order
    if residue == 0:
        return 0
    squares_list = [index * index % prime_order for index in range(1, prime_order)]
    return 1 if residue in squares_list else -1


def paley_matrix():
    prime_order = 13
    conference = np.zeros((14, 14))
    conference[0, 1:] = 1.0
    conference[1:, 0] = 1.0
    for row_index in range(prime_order):
        for col_index in range(prime_order):
            conference[row_index + 1, col_index + 1] = character(col_index - row_index, prime_order)
    first = np.array([[1.0, 1.0], [1.0, -1.0]])
    second = np.array([[1.0, -1.0], [-1.0, -1.0]])
    return np.kron(conference, first) + np.kron(np.eye(14), second)


def sylvester(order):
    matrix = np.ones((1, 1))
    basic = np.array([[1.0, 1.0], [1.0, -1.0]])
    while matrix.shape[0] < order:
        matrix = np.kron(basic, matrix)
    return matrix


def plan(levels):
    if levels == len(EXCHANGE[0]):
        return SIZES, EXCHANGE, REDUCE, zip(EVENTS, COSTS)
    plain = (tuple(range(levels)),) * 8
    stages = 2 * levels + 1
    turns = [turn - stage for turn in range(8 + stages) for stage in (*range(1, stages), 0)]
    turns = [chunk for chunk in turns if 0 <= chunk < 8]
    return (1,) * 8, plain, plain, [(chunk, 1) for chunk in turns]


def exchange(value, bit):
    pairs = [(source, source ^ (1 << bit)) for source in range(lax.axis_size("tensor"))]
    return lax.ppermute(value, "tensor", pairs)


def call(kernel, after, cost, operands, specs, outs, out_specs, grid, scratch=()):
    def run(_, *refs):
        kernel(*refs)

    return pl.pallas_call(
        run,
        out_shape=outs,
        grid=grid,
        in_specs=[pl.BlockSpec(memory_space=pl.ANY), *specs],
        out_specs=out_specs,
        scratch_shapes=list(scratch),
        compiler_params=pltpu.CompilerParams(vmem_limit_bytes=VMEM),
        cost_estimate=pl.CostEstimate(flops=cost, bytes_accessed=1, transcendentals=0),
    )(after, *operands)


def bf16(*shape):
    return jax.ShapeDtypeStruct(shape, jnp.bfloat16)


def rows_spec(rows, step, offset=0):
    return pl.BlockSpec((rows, step), lambda i: (i + offset, 0))


SCALAR = pl.BlockSpec(memory_space=pltpu.SMEM)


def activate(after, cost, gate, up, first, step):
    units = gate.shape[0]
    blocks = 4
    size = math.gcd(first, step)

    def kernel(gate_ref, up_ref, out_ref):
        g = gate_ref[...].astype(jnp.float32)
        u = up_ref[...].astype(jnp.float32)
        out_ref[...] = (0.5 * g * (1.0 + jnp.tanh(0.5 * g)) * u).astype(jnp.bfloat16)

    spec = pl.BlockSpec((units // blocks, size), lambda i, j: (i, first // size + j))
    return call(
        kernel, after, cost, (gate, up), [spec, spec], [bf16(units, step)],
        [pl.BlockSpec((units // blocks, size), lambda i, j: (i, j))], (blocks, step // size),
    )[0]


def mix(after, cost, partner, own, sign):
    units, step = own.shape
    blocks = 2

    def kernel(partner_ref, own_ref, sign_ref, out_ref):
        total = partner_ref[...].astype(jnp.float32) + sign_ref[0] * own_ref[...].astype(jnp.float32)
        out_ref[...] = total.astype(jnp.bfloat16)

    spec = rows_spec(units // blocks, step)
    return call(
        kernel, after, cost, (partner, own, sign), [spec, spec, SCALAR], [bf16(units, step)],
        [spec], (blocks,),
    )[0]


def project(after, cost, partner, own, sign, factor, weight, block_of, scale):
    units, step = own.shape
    features = weight.shape[1]
    blocks = block_of.shape[0] // 2
    rows = features // (2 * blocks)
    side = factor.shape[0]
    groups = units // side
    inner = side // 28

    def rotate(partner_ref, own_ref, sign_ref, factor_ref, rotated):
        total = partner_ref[...].astype(jnp.float32) + sign_ref[0] * own_ref[...].astype(jnp.float32)
        total = total.astype(jnp.bfloat16).reshape(28, groups, inner, step)
        parts = [
            jnp.dot(
                factor_ref[...], total[:, group].reshape(side, step), preferred_element_type=jnp.float32
            )
            for group in range(groups)
        ]
        distance = 1
        while distance < groups:
            parts = [
                parts[index] + parts[index ^ distance]
                if not index & distance
                else parts[index ^ distance] - parts[index]
                for index in range(groups)
            ]
            distance *= 2
        parts = [(part * scale).astype(jnp.bfloat16).reshape(28, 1, inner, step) for part in parts]
        rotated[...] = jnp.concatenate(parts, axis=1).reshape(units, step)

    def kernel(block_ref, _, partner_ref, own_ref, sign_ref, factor_ref, given_w, kept_w, given_ref, kept_ref, rotated):
        @pl.when(pl.program_id(0) == 0)
        def _():
            rotate(partner_ref, own_ref, sign_ref, factor_ref, rotated)

        for w_ref, out_ref in ((given_w, given_ref), (kept_w, kept_ref)):
            out_ref[...] = lax.dot_general(
                w_ref[...], rotated[...], (((0,), (0,)), ((), ())), preferred_element_type=jnp.float32
            ).astype(jnp.bfloat16)

    whole = pl.BlockSpec((units, step), lambda i, block: (0, 0))
    out = pl.BlockSpec((rows, step), lambda i, block: (i, 0))
    return pl.pallas_call(
        kernel,
        out_shape=[bf16(features // 2, step)] * 2,
        grid_spec=pltpu.PrefetchScalarGridSpec(
            num_scalar_prefetch=1,
            grid=(blocks,),
            in_specs=[
                pl.BlockSpec(memory_space=pl.ANY),
                whole,
                whole,
                SCALAR,
                pl.BlockSpec((side, side), lambda i, block: (0, 0)),
                pl.BlockSpec((units, rows), lambda i, block: (0, block[i])),
                pl.BlockSpec((units, rows), lambda i, block: (0, block[blocks + i])),
            ],
            out_specs=[out, out],
            scratch_shapes=[pltpu.VMEM((units, step), jnp.bfloat16)],
        ),
        compiler_params=pltpu.CompilerParams(vmem_limit_bytes=VMEM),
        cost_estimate=pl.CostEstimate(flops=cost, bytes_accessed=1, transcendentals=0),
    )(block_of, after, partner, own, sign, factor, weight, weight)


def add(after, cost, taken, kept):
    rows, step = kept.shape

    def kernel(taken_ref, kept_ref, out_ref):
        total = taken_ref[...].astype(jnp.float32) + kept_ref[...].astype(jnp.float32)
        out_ref[...] = total.astype(jnp.bfloat16)

    spec = rows_spec(rows, step)
    return call(kernel, after, cost, (taken, kept), [spec, spec], [bf16(rows, step)], [spec], (1,))[0]


def add_split(after, cost, taken, kept):
    rows, step = kept.shape
    half = rows // 2

    def kernel(taken_ref, kept_ref, given_ref, kept_out):
        total = taken_ref[...].astype(jnp.float32) + kept_ref[...].astype(jnp.float32)
        total = total.astype(jnp.bfloat16)
        kept_out[...] = total[:half]
        given_ref[...] = total[half:]

    spec = rows_spec(rows, step)
    out = rows_spec(half, step)
    return call(
        kernel, after, cost, (taken, kept), [spec, spec], [bf16(half, step)] * 2, [out, out], (1,)
    )


def body(gate_pre, up_pre, down_weight):
    left, width, tokens = gate_pre.shape
    units = left * width
    features = down_weight.shape[-1]
    devices = lax.axis_size("tensor")
    levels = devices.bit_length() - 1
    position = lax.axis_index("tensor")
    signs = [
        (1 - 2 * ((position >> level) & 1)).astype(jnp.float32).reshape(1) for level in range(levels)
    ]
    scale = 1.0 / math.sqrt(units * devices)
    inner = min(width, 16)
    factor = jnp.asarray(np.kron(paley_matrix(), sylvester(inner)), jnp.bfloat16)
    weight = down_weight.reshape(units, features)
    gate = gate_pre.reshape(units, tokens)
    up = up_pre.reshape(units, tokens)

    def blocks_of(reduction):
        order = sorted(
            range(devices),
            key=lambda r: (1 - (r >> reduction[0] & 1), *[r >> level & 1 for level in reduction[1:]]),
        )
        return jnp.asarray(order, jnp.int32) ^ position

    sizes, exchanges, reductions, turns = plan(levels)
    places = {reduction: blocks_of(reduction) for reduction in sorted(set(reductions))}
    stages = [0] * len(sizes)
    state = [None] * len(sizes)
    outs = [None] * len(sizes)
    last = gate
    for chunk, cost in turns:
        stage = stages[chunk]
        stages[chunk] += 1
        turn, reduction = exchanges[chunk], reductions[chunk]
        if stage == 0:
            step = tokens // sum(sizes)
            first = sum(sizes[:chunk])
            last = activate(last, cost, gate, up, first * step, sizes[chunk] * step)
            state[chunk] = (exchange(last, turn[0]), last)
            continue
        partner, own = state[chunk]
        if stage < levels:
            last = mix(last, cost, partner, own, signs[turn[stage - 1]])
            state[chunk] = (exchange(last, turn[stage]), last)
        elif stage == levels:
            given, last = project(
                last, cost, partner, own, signs[turn[-1]], factor, weight, places[reduction], scale
            )
            state[chunk] = (exchange(given, reduction[0]), last)
        elif stage < 2 * levels:
            given, last = add_split(last, cost, partner, own)
            state[chunk] = (exchange(given, reduction[stage - levels]), last)
        else:
            outs[chunk] = last = add(last, cost, partner, own)
    return jnp.concatenate(outs, axis=1)


def solution(mesh):
    in_specs = (P(None, "tensor", "dp"), P(None, "tensor", "dp"), P(None, "tensor", None))
    out_specs = P("tensor", "dp")
    return jax.shard_map(body, mesh=mesh, in_specs=in_specs, out_specs=out_specs, check_vma=False)
```

```python
import math

import jax
import jax.numpy as jnp
import numpy as np
from jax import lax
from jax.experimental import pallas as pl
from jax.experimental.pallas import tpu as pltpu
from jax.sharding import PartitionSpec as P

SIZES = (1, 1, 1, 1, 1, 1, 1, 1)
EXCHANGE = (
    (100, 101, 102, 0), (1, 0, 2), (0, 100, 101, 102), (0, 1, 2), (0, 2, 1), (100, 101, 102, 0), (2, 0, 1), (0, 1, 2),
)
REDUCE = (
    (0, 1, 2), (0, 1, 2), (0, 1, 2), (1, 0, 2), (0, 1, 2), (0, 2, 1), (0, 1, 2), (0, 1, 2),
)
EVENTS = (
    5, 7, 6, 2, 0, 5, 6, 7, 2, 0, 1, 4, 6, 3, 7, 5, 1, 3, 7, 2, 5, 3, 1, 0,
    7, 6, 3, 4, 0, 6, 7, 2, 3, 0, 6, 5, 3, 4, 2, 5, 0, 1, 4, 2, 6, 0, 5, 4,
    2, 3, 7, 1, 4, 0, 4, 1, 2, 5, 1,
)
COSTS = (
    1, 1, 1, 1, 1, 1048421339, 1, 1,
    1, 1, 1048421339, 2096842679, 1, 1, 1048421339, 1,
    1, 1, 1, 2096842679, 1048421339, 4193685358, 1, 1,
    1048421339, 1, 2096842679, 1, 4193685358, 1048421339, 4193685358, 1048421339,
    1048421339, 1048421339, 1048421339, 1, 1, 1, 1, 1048421339,
    1, 1, 1, 1, 1048421339, 1048421339, 2096842679, 1,
    1048421339, 2096842679, 1, 1, 1, 1048421339, 1048421339, 1,
    1048421339, 1, 1,
)
VMEM = 16 * 1024 * 1024


def character(value, prime_order):
    residue = value % prime_order
    if residue == 0:
        return 0
    squares_list = [index * index % prime_order for index in range(1, prime_order)]
    return 1 if residue in squares_list else -1


def paley_matrix():
    prime_order = 13
    conference = np.zeros((14, 14))
    conference[0, 1:] = 1.0
    conference[1:, 0] = 1.0
    for row_index in range(prime_order):
        for col_index in range(prime_order):
            conference[row_index + 1, col_index + 1] = character(col_index - row_index, prime_order)
    first = np.array([[1.0, 1.0], [1.0, -1.0]])
    second = np.array([[1.0, -1.0], [-1.0, -1.0]])
    return np.kron(conference, first) + np.kron(np.eye(14), second)


def sylvester(order):
    matrix = np.ones((1, 1))
    basic = np.array([[1.0, 1.0], [1.0, -1.0]])
    while matrix.shape[0] < order:
        matrix = np.kron(basic, matrix)
    return matrix


def plan(levels):
    if levels == len(REDUCE[0]):
        return SIZES, EXCHANGE, REDUCE, zip(EVENTS, COSTS)
    plain = (tuple(range(levels)),) * 8
    stages = 2 * levels + 1
    turns = [turn - stage for turn in range(8 + stages) for stage in (*range(1, stages), 0)]
    turns = [chunk for chunk in turns if 0 <= chunk < 8]
    return (1,) * 8, plain, plain, [(chunk, 1) for chunk in turns]


RELAY = 100


def exchange(value, step):
    size = lax.axis_size("tensor")
    if step < RELAY:
        pairs = [(source, source ^ (1 << step)) for source in range(size)]
    else:
        ends = [(near, near ^ 2) for near in range(size) if (near >> 1 & 1) == (near >> 2 & 1)]
        middle = [(near, near ^ 6) for near in range(size) if (near >> 1 & 1) != (near >> 2 & 1)]
        pairs = (ends, middle, [(to, end) for end, to in ends])[step - RELAY]
    return lax.ppermute(value, "tensor", pairs)


HELD = pl.BlockSpec(memory_space=pltpu.VMEM)
AWAY = pl.BlockSpec(memory_space=pltpu.HBM)


def call(kernel, after, cost, operands, specs, outs, scratch=()):
    def run(_, *refs):
        kernel(*refs)

    return pl.pallas_call(
        run,
        out_shape=[jax.ShapeDtypeStruct(shape, jnp.bfloat16) for shape in outs],
        in_specs=[pl.BlockSpec(memory_space=pl.ANY), *specs],
        out_specs=[HELD] * len(outs),
        scratch_shapes=list(scratch),
        compiler_params=pltpu.CompilerParams(vmem_limit_bytes=VMEM),
        cost_estimate=pl.CostEstimate(flops=cost, bytes_accessed=1, transcendentals=0),
    )(after, *operands)


def wide(ref):
    return ref[...].astype(jnp.float32)


def activate(after, cost, gate, up, first, step):
    units = gate.shape[0]
    blocks = 2
    rows = units // blocks

    def kernel(gate_ref, up_ref, out_ref, gates, ups, arrived):
        copies = [
            [
                pltpu.make_async_copy(
                    ref.at[pl.ds(block * rows, rows), pl.ds(first, step)],
                    held.at[block],
                    arrived.at[which, block],
                )
                for which, (ref, held) in enumerate(((gate_ref, gates), (up_ref, ups)))
            ]
            for block in range(blocks)
        ]
        for pair in copies:
            for copy in pair:
                copy.start()
        for block, pair in enumerate(copies):
            for copy in pair:
                copy.wait()
            g = gates[block].astype(jnp.float32)
            u = ups[block].astype(jnp.float32)
            out_ref[pl.ds(block * rows, rows), :] = (
                0.5 * g * (1.0 + jnp.tanh(0.5 * g)) * u
            ).astype(jnp.bfloat16)

    held = pltpu.VMEM((blocks, rows, step), jnp.bfloat16)
    return call(
        kernel, after, cost, (gate, up), [AWAY, AWAY], [(units, step)],
        [held, held, pltpu.SemaphoreType.DMA((2, blocks))],
    )[0]


def bit_of(level):
    return lax.axis_index("tensor") >> level & 1


def sign_of(level):
    return (1 - 2 * bit_of(level)).astype(jnp.float32)


def joined(partner_ref, own_ref, before):
    if before < RELAY:
        total = wide(partner_ref) + sign_of(before) * wide(own_ref)
    else:
        middle = bit_of(1) != bit_of(2)
        total = jnp.where(middle, wide(own_ref), wide(partner_ref))
    return total.astype(jnp.bfloat16)


def rows_of(units):
    size = math.gcd(units, 256)
    return [pl.ds(first, size) for first in range(0, units, size)]


def mix(after, cost, partner, own, before):
    def kernel(partner_ref, own_ref, out_ref):
        for rows in rows_of(own.shape[0]):
            out_ref[rows] = joined(partner_ref.at[rows], own_ref.at[rows], before)

    return call(kernel, after, cost, (partner, own), [HELD, HELD], [own.shape])[0]


def relay_sums(after, cost, partner, own):
    units, step = own.shape

    def kernel(partner_ref, own_ref, out_ref):
        sign = -sign_of(2)
        for rows in rows_of(units):
            there, here = wide(partner_ref.at[rows]), wide(own_ref.at[rows])
            out_ref[rows] = (here + there).astype(jnp.bfloat16)
            below = pl.ds(units + rows.start, rows.size)
            out_ref[below] = (sign * (here - there)).astype(jnp.bfloat16)

    return call(kernel, after, cost, (partner, own), [HELD, HELD], [(2 * units, step)])[0]


def relay_results(after, cost, partner, own):
    units, step = own.shape[0] // 2, own.shape[1]

    def kernel(partner_ref, own_ref, away_ref, kept_ref):
        lower, sign = bit_of(2) == 0, sign_of(2)
        for rows in rows_of(units):
            below = pl.ds(units + rows.start, rows.size)
            first, second = [
                (wide(partner_ref.at[part]) + sign * wide(own_ref.at[part])).astype(jnp.bfloat16)
                for part in (rows, below)
            ]
            away_ref[rows] = jnp.where(lower, first, second)
            kept_ref[rows] = jnp.where(lower, second, first)

    return call(kernel, after, cost, (partner, own), [HELD, HELD], [(units, step)] * 2)


def project(after, cost, partner, own, before, factor, weight, order, scale):
    units, step = own.shape
    features = weight.shape[1]
    count = len(order)
    rows = features // count
    side = factor.shape[0]
    groups = units // side
    inner = side // 28

    def kernel(partner_ref, own_ref, factor_ref, weight_ref, given_ref, kept_ref):
        position = lax.axis_index("tensor")
        total = joined(partner_ref, own_ref, before).reshape(28, groups, inner, step)
        parts = [
            jnp.dot(
                factor_ref[...], total[:, group].reshape(side, step), preferred_element_type=jnp.float32
            )
            for group in range(groups)
        ]
        distance = 1
        while distance < groups:
            parts = [
                parts[index] + parts[index ^ distance]
                if not index & distance
                else parts[index ^ distance] - parts[index]
                for index in range(groups)
            ]
            distance *= 2
        parts = [(part * scale).astype(jnp.bfloat16).reshape(28, 1, inner, step) for part in parts]
        rotated = jnp.concatenate(parts, axis=1).reshape(units, step).T
        for index, relative in enumerate(order):
            first = pl.multiple_of((position ^ relative) * rows, rows)
            product = jnp.dot(
                rotated, weight_ref[:, pl.ds(first, rows)], preferred_element_type=jnp.float32
            ).astype(jnp.bfloat16)
            out_ref = given_ref if index < count // 2 else kept_ref
            out_ref[:, index % (count // 2) * rows : (index % (count // 2) + 1) * rows] = product

    return call(
        kernel, after, cost, (partner, own, factor, weight),
        [HELD, HELD, HELD, HELD], [(step, features // 2)] * 2,
    )


def add(after, cost, taken, kept):
    step, rows = kept.shape

    def kernel(taken_ref, kept_ref, out_ref):
        out_ref[...] = (wide(taken_ref) + wide(kept_ref)).astype(jnp.bfloat16).T

    return call(kernel, after, cost, (taken, kept), [HELD, HELD], [(rows, step)])[0]


def add_split(after, cost, taken, kept):
    step, half = kept.shape[0], kept.shape[1] // 2

    def kernel(taken_ref, kept_ref, given_ref, kept_out):
        total = (wide(taken_ref) + wide(kept_ref)).astype(jnp.bfloat16)
        kept_out[...] = total[:, :half]
        given_ref[...] = total[:, half:]

    return call(kernel, after, cost, (taken, kept), [HELD, HELD], [(step, half)] * 2)


def body(gate_pre, up_pre, down_weight):
    left, width, tokens = gate_pre.shape
    units = left * width
    features = down_weight.shape[-1]
    devices = lax.axis_size("tensor")
    levels = devices.bit_length() - 1
    scale = 1.0 / math.sqrt(units * devices)
    inner = min(width, 16)
    factor = jnp.asarray(np.kron(paley_matrix(), sylvester(inner)), jnp.bfloat16)
    weight = down_weight.reshape(units, features)
    gate = gate_pre.reshape(units, tokens)
    up = up_pre.reshape(units, tokens)

    def order_of(reduction):
        return sorted(
            range(devices),
            key=lambda r: (1 - (r >> reduction[0] & 1), *[r >> level & 1 for level in reduction[1:]]),
        )

    sizes, exchanges, reductions, turns = plan(levels)
    stages = [0] * len(sizes)
    state = [None] * len(sizes)
    outs = [None] * len(sizes)
    last = gate
    for chunk, cost in turns:
        stage = stages[chunk]
        stages[chunk] += 1
        steps, reduction = exchanges[chunk], reductions[chunk]
        if stage == 0:
            step = tokens // sum(sizes)
            first = sum(sizes[:chunk])
            last = activate(last, cost, gate, up, first * step, sizes[chunk] * step)
            state[chunk] = (exchange(last, steps[0]), last)
            continue
        partner, own = state[chunk]
        before = steps[min(stage, len(steps)) - 1]
        if stage < len(steps):
            if before == RELAY:
                away = last = relay_sums(last, cost, partner, own)
            elif before == RELAY + 1:
                away, last = relay_results(last, cost, partner, own)
            else:
                away = last = mix(last, cost, partner, own, before)
            state[chunk] = (exchange(away, steps[stage]), last)
        elif stage == len(steps):
            given, last = project(
                last, cost, partner, own, before, factor, weight, order_of(reduction), scale
            )
            state[chunk] = (exchange(given, reduction[0]), last)
        elif stage < len(steps) + levels:
            given, last = add_split(last, cost, partner, own)
            state[chunk] = (exchange(given, reduction[stage - len(steps)]), last)
        else:
            outs[chunk] = last = add(last, cost, partner, own)
    return jnp.concatenate(outs, axis=1)


def solution(mesh):
    in_specs = (P(None, "tensor", "dp"), P(None, "tensor", "dp"), P(None, "tensor", None))
    out_specs = P("tensor", "dp")
    return jax.shard_map(body, mesh=mesh, in_specs=in_specs, out_specs=out_specs, check_vma=False)
```

```python
import math

import jax
import jax.numpy as jnp
import numpy as np
from jax import lax
from jax.experimental import pallas as pl
from jax.experimental.pallas import tpu as pltpu
from jax.sharding import PartitionSpec as P

SIZES = (1, 1, 1, 1, 1, 1, 1, 1)
EXCHANGE = (
    (0, 100, 101, 102), (0, 1, 2), (100, 101, 102, 0), (1, 0, 2), (2, 0, 1), (0, 100, 101, 102), (2, 0, 1), (0, 1, 2),
)
REDUCE = (
    (0, 1, 2), (0, 1, 2), (0, 1, 2), (0, 1, 2), (0, 1, 2), (0, 2, 1), (0, 1, 2), (1, 0, 2),
)
EVENTS = (
    4, 2, 0, 3, 5, 6, 7, 0, 4, 2, 7, 5, 6, 3, 4, 0, 6, 7, 1, 2, 3, 1, 6, 4,
    2, 6, 0, 3, 1, 2, 5, 3, 7, 2, 6, 3, 0, 5, 7, 0, 5, 4, 7, 2, 3, 1, 5, 0,
    7, 2, 1, 6, 4, 5, 1, 0, 4, 5, 1,
)
COSTS = (
    4193685358, 1, 1, 1, 4193685358, 1048421339, 1, 4193685358,
    1, 1048421339, 1, 1, 1, 8387370716, 1048421339, 1,
    4193685358, 1048421339, 2096842679, 8387370716, 2096842679, 8387370716, 1, 2096842679,
    4193685358, 2096842679, 1, 1, 2096842679, 8387370716, 4193685358, 8387370716,
    4193685358, 1, 1, 2096842679, 1048421339, 1, 1, 1,
    2096842679, 1048421339, 1048421339, 1, 1, 4193685358, 4193685358, 8387370716,
    1, 8387370716, 1, 8387370716, 4193685358, 1, 1, 2096842679,
    1, 1, 1,
)
VMEM = 16 * 1024 * 1024


def character(value, prime_order):
    residue = value % prime_order
    if residue == 0:
        return 0
    squares_list = [index * index % prime_order for index in range(1, prime_order)]
    return 1 if residue in squares_list else -1


def paley_matrix():
    prime_order = 13
    conference = np.zeros((14, 14))
    conference[0, 1:] = 1.0
    conference[1:, 0] = 1.0
    for row_index in range(prime_order):
        for col_index in range(prime_order):
            conference[row_index + 1, col_index + 1] = character(col_index - row_index, prime_order)
    first = np.array([[1.0, 1.0], [1.0, -1.0]])
    second = np.array([[1.0, -1.0], [-1.0, -1.0]])
    return np.kron(conference, first) + np.kron(np.eye(14), second)


def sylvester(order):
    matrix = np.ones((1, 1))
    basic = np.array([[1.0, 1.0], [1.0, -1.0]])
    while matrix.shape[0] < order:
        matrix = np.kron(basic, matrix)
    return matrix


def plan(levels):
    if levels == len(REDUCE[0]):
        return SIZES, EXCHANGE, REDUCE, zip(EVENTS, COSTS)
    plain = (tuple(range(levels)),) * 8
    stages = 2 * levels + 1
    turns = [turn - stage for turn in range(8 + stages) for stage in (*range(1, stages), 0)]
    turns = [chunk for chunk in turns if 0 <= chunk < 8]
    return (1,) * 8, plain, plain, [(chunk, 1) for chunk in turns]


RELAY = 100


def exchange(value, step):
    size = lax.axis_size("tensor")
    if step < RELAY:
        pairs = [(source, source ^ (1 << step)) for source in range(size)]
    else:
        ends = [(near, near ^ 2) for near in range(size) if (near >> 1 & 1) == (near >> 2 & 1)]
        middle = [(near, near ^ 6) for near in range(size) if (near >> 1 & 1) != (near >> 2 & 1)]
        pairs = (ends, middle, [(to, end) for end, to in ends])[step - RELAY]
    return lax.ppermute(value, "tensor", pairs)


HELD = pl.BlockSpec(memory_space=pltpu.VMEM)
AWAY = pl.BlockSpec(memory_space=pltpu.HBM)


def call(kernel, after, cost, operands, specs, outs, scratch=()):
    def run(_, *refs):
        kernel(*refs)

    return pl.pallas_call(
        run,
        out_shape=[jax.ShapeDtypeStruct(shape, jnp.bfloat16) for shape in outs],
        in_specs=[pl.BlockSpec(memory_space=pl.ANY), *specs],
        out_specs=[HELD] * len(outs),
        scratch_shapes=list(scratch),
        compiler_params=pltpu.CompilerParams(vmem_limit_bytes=VMEM),
        cost_estimate=pl.CostEstimate(flops=cost, bytes_accessed=1, transcendentals=0),
    )(after, *operands)


def wide(ref):
    return ref[...].astype(jnp.float32)


def activate(after, cost, gate, up, first, step):
    units = gate.shape[0]
    gate, up = gate[:, first : first + step], up[:, first : first + step]
    after = gate if after is None else after

    def kernel(gate_ref, up_ref, out_ref):
        for rows in rows_of(units):
            g, u = wide(gate_ref.at[rows]), wide(up_ref.at[rows])
            out_ref[rows] = (0.5 * g * (1.0 + jnp.tanh(0.5 * g)) * u).astype(jnp.bfloat16)

    return call(kernel, after, cost, (gate, up), [HELD, HELD], [(units, step)])[0]


def bit_of(level):
    return lax.axis_index("tensor") >> level & 1


def sign_of(level):
    return (1 - 2 * bit_of(level)).astype(jnp.float32)


def joined(partner_ref, own_ref, before):
    if before < RELAY:
        total = wide(partner_ref) + sign_of(before) * wide(own_ref)
    else:
        middle = bit_of(1) != bit_of(2)
        total = jnp.where(middle, wide(own_ref), wide(partner_ref))
    return total.astype(jnp.bfloat16)


def rows_of(units):
    size = math.gcd(units, 256)
    return [pl.ds(first, size) for first in range(0, units, size)]


def mix(after, cost, partner, own, before):
    def kernel(partner_ref, own_ref, out_ref):
        for rows in rows_of(own.shape[0]):
            out_ref[rows] = joined(partner_ref.at[rows], own_ref.at[rows], before)

    return call(kernel, after, cost, (partner, own), [HELD, HELD], [own.shape])[0]


def relay_sums(after, cost, partner, own):
    units, step = own.shape

    def kernel(partner_ref, own_ref, out_ref):
        sign = -sign_of(2)
        for rows in rows_of(units):
            there, here = wide(partner_ref.at[rows]), wide(own_ref.at[rows])
            out_ref[rows] = (here + there).astype(jnp.bfloat16)
            below = pl.ds(units + rows.start, rows.size)
            out_ref[below] = (sign * (here - there)).astype(jnp.bfloat16)

    return call(kernel, after, cost, (partner, own), [HELD, HELD], [(2 * units, step)])[0]


def relay_results(after, cost, partner, own):
    units, step = own.shape[0] // 2, own.shape[1]

    def kernel(partner_ref, own_ref, away_ref, kept_ref):
        lower, sign = bit_of(2) == 0, sign_of(2)
        for rows in rows_of(units):
            below = pl.ds(units + rows.start, rows.size)
            first, second = [
                (wide(partner_ref.at[part]) + sign * wide(own_ref.at[part])).astype(jnp.bfloat16)
                for part in (rows, below)
            ]
            away_ref[rows] = jnp.where(lower, first, second)
            kept_ref[rows] = jnp.where(lower, second, first)

    return call(kernel, after, cost, (partner, own), [HELD, HELD], [(units, step)] * 2)


def project(after, cost, partner, own, before, factor, weight, order, scale):
    units, step = own.shape
    features = weight.shape[1]
    count = len(order)
    rows = features // count
    side = factor.shape[0]
    groups = units // side
    inner = side // 28

    def kernel(partner_ref, own_ref, factor_ref, weight_ref, given_ref, kept_ref):
        position = lax.axis_index("tensor")
        total = joined(partner_ref, own_ref, before).reshape(28, groups, inner, step)
        parts = [
            jnp.dot(
                factor_ref[...], total[:, group].reshape(side, step), preferred_element_type=jnp.float32
            )
            for group in range(groups)
        ]
        distance = 1
        while distance < groups:
            parts = [
                parts[index] + parts[index ^ distance]
                if not index & distance
                else parts[index ^ distance] - parts[index]
                for index in range(groups)
            ]
            distance *= 2
        parts = [(part * scale).astype(jnp.bfloat16).reshape(28, 1, inner, step) for part in parts]
        rotated = jnp.concatenate(parts, axis=1).reshape(units, step).T
        for index, relative in enumerate(order):
            first = pl.multiple_of((position ^ relative) * rows, rows)
            product = jnp.dot(
                rotated, weight_ref[:, pl.ds(first, rows)], preferred_element_type=jnp.float32
            ).astype(jnp.bfloat16)
            out_ref = given_ref if index < count // 2 else kept_ref
            out_ref[:, index % (count // 2) * rows : (index % (count // 2) + 1) * rows] = product

    return call(
        kernel, after, cost, (partner, own, factor, weight),
        [HELD, HELD, HELD, HELD], [(step, features // 2)] * 2,
    )


def add(after, cost, taken, kept, whole, first, tokens):
    step, rows = kept.shape

    def kernel(_, taken_ref, kept_ref, *refs):
        whole_ref, token_ref, block, done = refs[-4:]
        block[...] = (wide(taken_ref) + wide(kept_ref)).astype(jnp.bfloat16).T
        token_ref[...] = jnp.zeros_like(token_ref)
        copy = pltpu.make_async_copy(block, whole_ref.at[:, pl.ds(first, step)], done)
        copy.start()
        copy.wait()

    more = () if whole is None else (whole,)
    return pl.pallas_call(
        kernel,
        out_shape=[
            jax.ShapeDtypeStruct((rows, tokens), jnp.bfloat16),
            jax.ShapeDtypeStruct((16, 128), jnp.bfloat16),
        ],
        in_specs=[pl.BlockSpec(memory_space=pl.ANY), HELD, HELD, *[AWAY for _ in more]],
        out_specs=[AWAY, HELD],
        scratch_shapes=[pltpu.VMEM((rows, step), jnp.bfloat16), pltpu.SemaphoreType.DMA(())],
        input_output_aliases={3: 0} if more else {},
        compiler_params=pltpu.CompilerParams(vmem_limit_bytes=VMEM),
        cost_estimate=pl.CostEstimate(flops=cost, bytes_accessed=1, transcendentals=0),
    )(after, taken, kept, *more)


def add_split(after, cost, taken, kept):
    step, half = kept.shape[0], kept.shape[1] // 2

    def kernel(taken_ref, kept_ref, given_ref, kept_out):
        total = (wide(taken_ref) + wide(kept_ref)).astype(jnp.bfloat16)
        kept_out[...] = total[:, :half]
        given_ref[...] = total[:, half:]

    return call(kernel, after, cost, (taken, kept), [HELD, HELD], [(step, half)] * 2)


def body(gate_pre, up_pre, down_weight):
    left, width, tokens = gate_pre.shape
    units = left * width
    features = down_weight.shape[-1]
    devices = lax.axis_size("tensor")
    levels = devices.bit_length() - 1
    scale = 1.0 / math.sqrt(units * devices)
    inner = min(width, 16)
    factor = jnp.asarray(np.kron(paley_matrix(), sylvester(inner)), jnp.bfloat16)
    weight = down_weight.reshape(units, features)
    gate = gate_pre.reshape(units, tokens)
    up = up_pre.reshape(units, tokens)

    def order_of(reduction):
        return sorted(
            range(devices),
            key=lambda r: (1 - (r >> reduction[0] & 1), *[r >> level & 1 for level in reduction[1:]]),
        )

    sizes, exchanges, reductions, turns = plan(levels)
    stages = [0] * len(sizes)
    state = [None] * len(sizes)
    whole = last = None
    for chunk, cost in turns:
        stage = stages[chunk]
        stages[chunk] += 1
        steps, reduction = exchanges[chunk], reductions[chunk]
        if stage == 0:
            step = tokens // sum(sizes)
            first = sum(sizes[:chunk])
            last = activate(last, cost, gate, up, first * step, sizes[chunk] * step)
            if stages.count(0) == len(sizes) - 1:
                gate, up, last = lax.optimization_barrier((gate, up, last))
            state[chunk] = (exchange(last, steps[0]), last)
            continue
        partner, own = state[chunk]
        before = steps[min(stage, len(steps)) - 1]
        if stage < len(steps):
            if before == RELAY:
                away = last = relay_sums(last, cost, partner, own)
            elif before == RELAY + 1:
                away, last = relay_results(last, cost, partner, own)
            else:
                away = last = mix(last, cost, partner, own, before)
            state[chunk] = (exchange(away, steps[stage]), last)
        elif stage == len(steps):
            given, last = project(
                last, cost, partner, own, before, factor, weight, order_of(reduction), scale
            )
            state[chunk] = (exchange(given, reduction[0]), last)
        elif stage < len(steps) + levels:
            given, last = add_split(last, cost, partner, own)
            state[chunk] = (exchange(given, reduction[stage - len(steps)]), last)
        else:
            first = sum(sizes[:chunk]) * (tokens // sum(sizes))
            whole, last = add(last, cost, partner, own, whole, first, tokens)
    return whole


def solution(mesh):
    in_specs = (P(None, "tensor", "dp"), P(None, "tensor", "dp"), P(None, "tensor", None))
    out_specs = P("tensor", "dp")
    return jax.shard_map(body, mesh=mesh, in_specs=in_specs, out_specs=out_specs, check_vma=False)
```

```python
import math

import jax
import jax.numpy as jnp
import numpy as np
from jax import lax
from jax.experimental import pallas as pl
from jax.experimental.pallas import tpu as pltpu
from jax.sharding import PartitionSpec as P

SIZES = (1, 1, 1, 1, 1, 1, 1, 1)
EXCHANGE = (
    (0, 100, 101, 102), (0, 1, 2), (100, 101, 102, 0), (1, 0, 2), (2, 0, 1), (0, 100, 101, 102), (2, 0, 1), (0, 1, 2),
)
REDUCE = (
    (0, 1, 2), (0, 1, 2), (0, 1, 2), (0, 1, 2), (0, 1, 2), (0, 2, 1), (0, 1, 2), (1, 0, 2),
)
EVENTS = (
    4, 2, 0, 3, 5, 6, 7, 0, 4, 2, 7, 5, 6, 3, 4, 0, 6, 7, 1, 2, 3, 1, 6, 4,
    2, 6, 0, 3, 1, 2, 5, 3, 7, 2, 6, 3, 0, 5, 7, 0, 5, 4, 7, 2, 3, 1, 5, 0,
    7, 2, 1, 6, 4, 5, 1, 0, 4, 5, 1,
)
COSTS = (
    4193685358, 1, 1, 1, 4193685358, 1048421339, 1, 4193685358,
    1, 1048421339, 1, 1, 1, 8387370716, 1048421339, 1,
    4193685358, 1048421339, 2096842679, 8387370716, 2096842679, 8387370716, 1, 2096842679,
    4193685358, 2096842679, 1, 1, 2096842679, 8387370716, 4193685358, 8387370716,
    4193685358, 1, 1, 2096842679, 1048421339, 1, 1, 1,
    2096842679, 1048421339, 1048421339, 1, 1, 4193685358, 4193685358, 8387370716,
    1, 8387370716, 1, 8387370716, 4193685358, 1, 1, 2096842679,
    1, 1, 1,
)
VMEM = 16 * 1024 * 1024


def character(value, prime_order):
    residue = value % prime_order
    if residue == 0:
        return 0
    squares_list = [index * index % prime_order for index in range(1, prime_order)]
    return 1 if residue in squares_list else -1


def paley_matrix():
    prime_order = 13
    conference = np.zeros((14, 14))
    conference[0, 1:] = 1.0
    conference[1:, 0] = 1.0
    for row_index in range(prime_order):
        for col_index in range(prime_order):
            conference[row_index + 1, col_index + 1] = character(col_index - row_index, prime_order)
    first = np.array([[1.0, 1.0], [1.0, -1.0]])
    second = np.array([[1.0, -1.0], [-1.0, -1.0]])
    return np.kron(conference, first) + np.kron(np.eye(14), second)


def sylvester(order):
    matrix = np.ones((1, 1))
    basic = np.array([[1.0, 1.0], [1.0, -1.0]])
    while matrix.shape[0] < order:
        matrix = np.kron(basic, matrix)
    return matrix


def plan(levels):
    if levels == len(REDUCE[0]):
        return SIZES, EXCHANGE, REDUCE, zip(EVENTS, COSTS)
    plain = (tuple(range(levels)),) * 8
    stages = 2 * levels + 1
    turns = [turn - stage for turn in range(8 + stages) for stage in (*range(1, stages), 0)]
    turns = [chunk for chunk in turns if 0 <= chunk < 8]
    return (1,) * 8, plain, plain, [(chunk, 1) for chunk in turns]


RELAY = 100


def exchange(value, step):
    size = lax.axis_size("tensor")
    if step < RELAY:
        pairs = [(source, source ^ (1 << step)) for source in range(size)]
    else:
        ends = [(near, near ^ 2) for near in range(size) if (near >> 1 & 1) == (near >> 2 & 1)]
        middle = [(near, near ^ 6) for near in range(size) if (near >> 1 & 1) != (near >> 2 & 1)]
        pairs = (ends, middle, [(to, end) for end, to in ends])[step - RELAY]
    return lax.ppermute(value, "tensor", pairs)


HELD = pl.BlockSpec(memory_space=pltpu.VMEM)
AWAY = pl.BlockSpec(memory_space=pltpu.HBM)


def call(kernel, after, cost, operands, specs, outs, scratch=()):
    def run(_, *refs):
        kernel(*refs)

    return pl.pallas_call(
        run,
        out_shape=[jax.ShapeDtypeStruct(shape, jnp.bfloat16) for shape in outs],
        in_specs=[pl.BlockSpec(memory_space=pl.ANY), *specs],
        out_specs=[HELD] * len(outs),
        scratch_shapes=list(scratch),
        compiler_params=pltpu.CompilerParams(vmem_limit_bytes=VMEM),
        cost_estimate=pl.CostEstimate(flops=cost, bytes_accessed=1, transcendentals=0),
    )(after, *operands)


def wide(ref):
    return ref[...].astype(jnp.float32)


def activate(after, cost, gate, up, first, step):
    units = gate.shape[0]
    gate, up = gate[:, first : first + step], up[:, first : first + step]

    def kernel(gate_ref, up_ref, out_ref):
        for rows in rows_of(units):
            g, u = wide(gate_ref.at[rows]), wide(up_ref.at[rows])
            out_ref[rows] = (0.5 * g * (1.0 + jnp.tanh(0.5 * g)) * u).astype(jnp.bfloat16)

    return call(kernel, after, cost, (gate, up), [HELD, HELD], [(units, step)])[0]


def bit_of(level):
    return lax.axis_index("tensor") >> level & 1


def sign_of(level):
    return (1 - 2 * bit_of(level)).astype(jnp.float32)


def joined(partner_ref, own_ref, before):
    if before < RELAY:
        total = wide(partner_ref) + sign_of(before) * wide(own_ref)
    else:
        middle = bit_of(1) != bit_of(2)
        total = jnp.where(middle, wide(own_ref), wide(partner_ref))
    return total.astype(jnp.bfloat16)


def rows_of(units):
    size = math.gcd(units, 256)
    return [pl.ds(first, size) for first in range(0, units, size)]


def mix(after, cost, partner, own, before):
    def kernel(partner_ref, own_ref, out_ref):
        for rows in rows_of(own.shape[0]):
            out_ref[rows] = joined(partner_ref.at[rows], own_ref.at[rows], before)

    return call(kernel, after, cost, (partner, own), [HELD, HELD], [own.shape])[0]


def relay_sums(after, cost, partner, own):
    units, step = own.shape

    def kernel(partner_ref, own_ref, out_ref):
        sign = -sign_of(2)
        for rows in rows_of(units):
            there, here = wide(partner_ref.at[rows]), wide(own_ref.at[rows])
            out_ref[rows] = (here + there).astype(jnp.bfloat16)
            below = pl.ds(units + rows.start, rows.size)
            out_ref[below] = (sign * (here - there)).astype(jnp.bfloat16)

    return call(kernel, after, cost, (partner, own), [HELD, HELD], [(2 * units, step)])[0]


def relay_results(after, cost, partner, own):
    units, step = own.shape[0] // 2, own.shape[1]

    def kernel(partner_ref, own_ref, away_ref, kept_ref):
        lower, sign = bit_of(2) == 0, sign_of(2)
        for rows in rows_of(units):
            below = pl.ds(units + rows.start, rows.size)
            first, second = [
                (wide(partner_ref.at[part]) + sign * wide(own_ref.at[part])).astype(jnp.bfloat16)
                for part in (rows, below)
            ]
            away_ref[rows] = jnp.where(lower, first, second)
            kept_ref[rows] = jnp.where(lower, second, first)

    return call(kernel, after, cost, (partner, own), [HELD, HELD], [(units, step)] * 2)


def project(after, cost, partner, own, before, factor, weight, order, scale):
    units, step = own.shape
    features = weight.shape[1]
    count = len(order)
    rows = features // count
    side = factor.shape[0]
    groups = units // side
    inner = side // 28

    def kernel(partner_ref, own_ref, factor_ref, weight_ref, given_ref, kept_ref):
        position = lax.axis_index("tensor")
        total = joined(partner_ref, own_ref, before).reshape(28, groups, inner, step)
        parts = [
            jnp.dot(
                factor_ref[...], total[:, group].reshape(side, step), preferred_element_type=jnp.float32
            )
            for group in range(groups)
        ]
        distance = 1
        while distance < groups:
            parts = [
                parts[index] + parts[index ^ distance]
                if not index & distance
                else parts[index ^ distance] - parts[index]
                for index in range(groups)
            ]
            distance *= 2
        parts = [(part * scale).astype(jnp.bfloat16).reshape(28, 1, inner, step) for part in parts]
        rotated = jnp.concatenate(parts, axis=1).reshape(units, step).T
        for index, relative in enumerate(order):
            first = pl.multiple_of((position ^ relative) * rows, rows)
            product = jnp.dot(
                rotated, weight_ref[:, pl.ds(first, rows)], preferred_element_type=jnp.float32
            ).astype(jnp.bfloat16)
            out_ref = given_ref if index < count // 2 else kept_ref
            out_ref[:, index % (count // 2) * rows : (index % (count // 2) + 1) * rows] = product

    return call(
        kernel, after, cost, (partner, own, factor, weight),
        [HELD, HELD, HELD, HELD], [(step, features // 2)] * 2,
    )


def add(after, cost, taken, kept, whole, first, tokens):
    step, rows = kept.shape

    def kernel(_, taken_ref, kept_ref, *refs):
        whole_ref, token_ref, block, done = refs[-4:]
        block[...] = (wide(taken_ref) + wide(kept_ref)).astype(jnp.bfloat16).T
        token_ref[...] = jnp.zeros_like(token_ref)
        copy = pltpu.make_async_copy(block, whole_ref.at[:, pl.ds(first, step)], done)
        copy.start()
        copy.wait()

    more = () if whole is None else (whole,)
    return pl.pallas_call(
        kernel,
        out_shape=[
            jax.ShapeDtypeStruct((rows, tokens), jnp.bfloat16),
            jax.ShapeDtypeStruct((16, 128), jnp.bfloat16),
        ],
        in_specs=[pl.BlockSpec(memory_space=pl.ANY), HELD, HELD, *[AWAY for _ in more]],
        out_specs=[AWAY, HELD],
        scratch_shapes=[pltpu.VMEM((rows, step), jnp.bfloat16), pltpu.SemaphoreType.DMA(())],
        input_output_aliases={3: 0} if more else {},
        compiler_params=pltpu.CompilerParams(vmem_limit_bytes=VMEM),
        cost_estimate=pl.CostEstimate(flops=cost, bytes_accessed=1, transcendentals=0),
    )(after, taken, kept, *more)


def add_split(after, cost, taken, kept):
    step, half = kept.shape[0], kept.shape[1] // 2

    def kernel(taken_ref, kept_ref, given_ref, kept_out):
        total = (wide(taken_ref) + wide(kept_ref)).astype(jnp.bfloat16)
        kept_out[...] = total[:, :half]
        given_ref[...] = total[:, half:]

    return call(kernel, after, cost, (taken, kept), [HELD, HELD], [(step, half)] * 2)


def body(gate_pre, up_pre, down_weight):
    left, width, tokens = gate_pre.shape
    units = left * width
    features = down_weight.shape[-1]
    devices = lax.axis_size("tensor")
    levels = devices.bit_length() - 1
    scale = 1.0 / math.sqrt(units * devices)
    inner = min(width, 16)
    factor = jnp.asarray(np.kron(paley_matrix(), sylvester(inner)), jnp.bfloat16)
    weight = down_weight.reshape(units, features)
    gate = gate_pre.reshape(units, tokens)
    up = up_pre.reshape(units, tokens)

    def order_of(reduction):
        return sorted(
            range(devices),
            key=lambda r: (1 - (r >> reduction[0] & 1), *[r >> level & 1 for level in reduction[1:]]),
        )

    sizes, exchanges, reductions, turns = plan(levels)
    stages = [0] * len(sizes)
    state = [None] * len(sizes)
    whole = last = None
    for chunk, cost in turns:
        stage = stages[chunk]
        stages[chunk] += 1
        steps, reduction = exchanges[chunk], reductions[chunk]
        if stage == 0:
            step = tokens // sum(sizes)
            first = sum(sizes[:chunk])
            if last is None:
                part = slice(first * step, (first + sizes[chunk]) * step)
                g, u = gate[:, part].astype(jnp.float32), up[:, part].astype(jnp.float32)
                last = (0.5 * g * (1.0 + jnp.tanh(0.5 * g)) * u).astype(jnp.bfloat16)
            else:
                last = activate(last, cost, gate, up, first * step, sizes[chunk] * step)
            if stages.count(0) == len(sizes) - 1:
                gate, up, last = lax.optimization_barrier((gate, up, last))
            state[chunk] = (exchange(last, steps[0]), last)
            continue
        partner, own = state[chunk]
        before = steps[min(stage, len(steps)) - 1]
        if stage < len(steps):
            if before == RELAY:
                away = last = relay_sums(last, cost, partner, own)
            elif before == RELAY + 1:
                away, last = relay_results(last, cost, partner, own)
            else:
                away = last = mix(last, cost, partner, own, before)
            state[chunk] = (exchange(away, steps[stage]), last)
        elif stage == len(steps):
            given, last = project(
                last, cost, partner, own, before, factor, weight, order_of(reduction), scale
            )
            state[chunk] = (exchange(given, reduction[0]), last)
        elif stage < len(steps) + levels:
            given, last = add_split(last, cost, partner, own)
            state[chunk] = (exchange(given, reduction[stage - len(steps)]), last)
        else:
            first = sum(sizes[:chunk]) * (tokens // sum(sizes))
            whole, last = add(last, cost, partner, own, whole, first, tokens)
    return whole


def solution(mesh):
    in_specs = (P(None, "tensor", "dp"), P(None, "tensor", "dp"), P(None, "tensor", None))
    out_specs = P("tensor", "dp")
    return jax.shard_map(body, mesh=mesh, in_specs=in_specs, out_specs=out_specs, check_vma=False)
```
